128 devices in a mesh: rep: 8 (over z, x_lo), feat: 16 (over x_hi, y, core).
Axes of the slice: x: 4 (x_hi: 2, x_lo: 2; x = x_hi * 2 + x_lo), y: 4, z: 4, core: 2. Of those that a mesh axis runs over, the one named last changes fastest.
Arguments:
- hidden: bfloat16 [4, 8192, 4096], P(None, 'rep', 'feat'), may hold values from -6 to 6
- labels: int32 [4, 8192, 1024], P(None, 'rep'), may hold values 0 or 1
- weights: float32 [8, 4096, 1024], P('rep', 'feat'), may hold values from -0.09375 to 0.09375
Outputs:
- trained: float32 [8, 4096, 1024], P('rep', 'feat')
The draws below stay inside these ranges and needn't reach their ends.
All inputs are finite; a program needn't handle non-finite values. No bound on the sum of `labels` on one device may be relied on, other than what follows from the above.
Results may differ from the reference program's by a relative error of at most 0.0009.
Values sent between devices are 32-bit elements; how exact they have to be, the bound alone decides.
No kernel may reach another device: no remote copies, remote signals or barrier semaphores. Data moves between devices by JAX's collectives and lax.ppermute only.
A program may use at most 128 MiB of HBM per device.

```python
import jax
import jax.numpy as jnp
from jax import lax

D = 4096
PROBES = 1024
ROWS = 1024
STEPS = 4
REPS = 8
ALLROWS = 8192
N_REP = 8


def with_ends(drawn, own_key, smallest, high):
    dims = drawn.shape
    place = [jax.random.randint(jax.random.fold_in(own_key, axis), (), 0, dims[axis]) for axis in range(len(dims))]
    drawn = drawn.at[tuple(place)].set(smallest)
    longest = dims.index(max(dims))
    place[longest] = (place[longest] + 1) % dims[longest]
    return drawn.at[tuple(place)].set(high)


def block_levels(rng, dims, split, least, top_value):
    level = 1.0
    for position, shards_of in split:
        heights = jax.random.uniform(jax.random.fold_in(jax.random.fold_in(rng, 6), position), (shards_of,), jnp.float32, least / len(split), top_value / len(split))
        level = level * jnp.repeat(jnp.exp(heights), dims[position] // shards_of).reshape((-1,) + (1,) * (len(dims) - 1 - position))
    return level


def centred(key, dims, width, most, split=(), held_as=jnp.bfloat16):
    level = block_levels(key, dims, split, -0.22, 0.18) if split else 1.0
    result = jax.random.normal(key, dims, jnp.float32) * width * level
    return jnp.minimum(jnp.maximum(result, -most), most).astype(held_as)


def setup_inputs(seed: int = 0) -> dict:
    seeds = jax.random.split(jax.random.key(seed), 4)
    hidden = centred(seeds[0], (STEPS, ALLROWS, D), 1.0, 6.0, ((1, 8), (2, 16)))
    labels = with_ends((jax.random.randint(seeds[1], (STEPS, ALLROWS, PROBES), 0, 3) < 1).astype(jnp.int32), jax.random.fold_in(seeds[1], 1), 0, 1)
    weights = centred(seeds[2], (REPS, D, PROBES), D ** -0.5, 0.09375, ((0, 8), (1, 16)), jnp.float32)
    return dict(hidden=hidden, labels=labels, weights=weights)


def reference(hidden, labels, weights):
    bits = N_REP.bit_length() - 1
    state = weights
    for step in range(STEPS):
        rows = hidden[step].reshape(N_REP, ROWS, D).astype(jnp.float32)
        targets = labels[step].reshape(N_REP, ROWS, PROBES).astype(jnp.float32)
        margin = jnp.einsum("rnd,rdp->rnp", rows, state, precision=lax.Precision.HIGHEST)
        residual = jax.nn.sigmoid(margin) - targets
        grad = jnp.einsum("rnd,rnp->rdp", rows, residual, precision=lax.Precision.HIGHEST)
        update = state - (2.0 / ROWS) * grad
        partner = jnp.arange(N_REP, dtype=jnp.int32) ^ (1 << (step % bits))
        state = 0.5 * (update + update[partner])
    return state
```

```python
import jax
import jax.numpy as jnp
import numpy as np
from jax import lax
from jax.experimental import pallas as pl
from jax.experimental.pallas import tpu as pltpu
from jax.sharding import Mesh, PartitionSpec as P

STEPS = 4
Y, CORES = 4, 2
LANES = Y * CORES


def xor_perm(size, mask):
    return [(i, i ^ mask) for i in range(size)]


def widen(hidden):
    steps, rows, feats = hidden.shape

    def body(x_ref, o_ref):
        o_ref[...] = x_ref[...].astype(jnp.float32)

    spec = pl.BlockSpec((1, rows, feats), lambda s: (s, 0, 0))
    return pl.pallas_call(
        body,
        grid=(steps,),
        in_specs=[spec],
        out_specs=spec,
        out_shape=jax.ShapeDtypeStruct(hidden.shape, jnp.float32),
    )(hidden)


def narrow(blocks, order):
    count, rows, feats = blocks.shape

    def body(order_ref, x_ref, o_ref):
        o_ref[...] = x_ref[0].astype(jnp.bfloat16)

    return pl.pallas_call(
        body,
        grid_spec=pltpu.PrefetchScalarGridSpec(
            num_scalar_prefetch=1,
            grid=(count,),
            in_specs=[pl.BlockSpec((1, rows, feats), lambda i, order: (order[i], 0, 0))],
            out_specs=pl.BlockSpec((rows, feats), lambda i, order: (0, i)),
        ),
        out_shape=jax.ShapeDtypeStruct((rows, count * feats), jnp.bfloat16),
    )(order, blocks)


def weights_in(weights, order):
    feats, probes = weights.shape
    width = probes // LANES

    def body(order_ref, w_ref, o_ref):
        o_ref[0] = w_ref[...].T

    return pl.pallas_call(
        body,
        grid_spec=pltpu.PrefetchScalarGridSpec(
            num_scalar_prefetch=1,
            grid=(LANES,),
            in_specs=[pl.BlockSpec((feats, width), lambda i, order: (0, order[i]))],
            out_specs=pl.BlockSpec((1, width, feats), lambda i, order: (i, 0, 0)),
        ),
        out_shape=jax.ShapeDtypeStruct((LANES, width, feats), jnp.float32),
    )(order, weights)


def weights_out(blocks, order):
    _, width, feats = blocks.shape

    def body(order_ref, w_ref, o_ref):
        o_ref[...] = w_ref[0].T

    return pl.pallas_call(
        body,
        grid_spec=pltpu.PrefetchScalarGridSpec(
            num_scalar_prefetch=1,
            grid=(LANES,),
            in_specs=[pl.BlockSpec((1, width, feats), lambda i, order: (i, 0, 0))],
            out_specs=pl.BlockSpec((feats, width), lambda i, order: (0, order[i])),
        ),
        out_shape=jax.ShapeDtypeStruct((feats, LANES * width), jnp.float32),
    )(order, blocks)


def labels_in(labels, order):
    steps, rows, probes = labels.shape
    width = probes // LANES

    def body(order_ref, l_ref, o_ref):
        o_ref[0] = l_ref[0].astype(jnp.float32).T

    return pl.pallas_call(
        body,
        grid_spec=pltpu.PrefetchScalarGridSpec(
            num_scalar_prefetch=1,
            grid=(steps,),
            in_specs=[pl.BlockSpec((1, rows, width), lambda s, order: (s, 0, order[0]))],
            out_specs=pl.BlockSpec((1, width, rows), lambda s, order: (s, 0, 0)),
        ),
        out_shape=jax.ShapeDtypeStruct((steps, width, rows), jnp.float32),
    )(order, labels)


def pieces(x):
    high = lax.reduce_precision(x, 8, 7)
    return jnp.concatenate([high.astype(jnp.bfloat16), (x - high).astype(jnp.bfloat16)])


def two_pass(x, y, dims):
    n = x.shape[0]
    out = lax.dot_general(pieces(x), y, dims, preferred_element_type=jnp.float32)
    return out[:n] + out[n:]


def gather_first(x):
    half = x.shape[0] // 2
    one = lax.ppermute(x, "y", xor_perm(Y, 1))
    three = lax.ppermute(x, "y", xor_perm(Y, 3))
    two = jnp.concatenate(
        [
            lax.ppermute(one[:half], "y", xor_perm(Y, 3)),
            lax.ppermute(three[half:], "y", xor_perm(Y, 1)),
        ]
    )
    own = jnp.stack([x, one, two, three])
    other = lax.ppermute(own, "core", xor_perm(CORES, 1))
    return jnp.stack([own, other], axis=1).reshape((LANES,) + x.shape)


def local(hidden, labels, weights):
    rows, feats = hidden.shape[1:]
    y, core = lax.axis_index("y"), lax.axis_index("core")
    order = jnp.stack(
        [(y ^ k) * CORES + (core ^ j) for k in range(Y) for j in range(CORES)]
    ).astype(jnp.int32)
    straight = jnp.arange(LANES, dtype=jnp.int32)

    wide = widen(hidden)
    first = gather_first(wide[0])

    blocks = weights_in(weights[0], order).reshape(Y, CORES, -1, feats)
    width = blocks.shape[2]
    other = lax.ppermute(blocks[:, 1], "core", xor_perm(CORES, 1))
    blocks = jnp.concatenate([blocks[:, 0], other], axis=-1)
    state = jnp.concatenate(
        [blocks[0]] + [lax.ppermute(blocks[k], "y", xor_perm(Y, k)) for k in (1, 2, 3)], axis=-1
    )

    targets = labels_in(labels, order)
    later = [lax.all_gather(wide[s], ("y", "core")) for s in range(1, STEPS)]

    for step in range(STEPS):
        x = narrow(first, straight) if step == 0 else narrow(later[step - 1], order)
        partial_margin = two_pass(state, x, (((1,), (1,)), ((), ())))
        margin = partial_margin + lax.ppermute(partial_margin, "x_hi", xor_perm(2, 1))
        residual = jax.nn.sigmoid(margin) - targets[step]
        grad = two_pass(residual, x, (((1,), (0,)), ((), ())))
        update = state - 2.0 / rows * grad
        bit = step % 3
        if bit == 0:
            partner = lax.ppermute(update, "x_lo", xor_perm(2, 1))
        else:
            partner = lax.ppermute(update, "z", xor_perm(4, bit))
        state = 0.5 * (update + partner)

    blocks = state.reshape(width, Y, CORES * feats)
    blocks = jnp.stack(
        [blocks[:, 0]] + [lax.ppermute(blocks[:, k], "y", xor_perm(Y, k)) for k in (1, 2, 3)]
    ).reshape(Y, width, CORES, feats)
    other = lax.ppermute(blocks[:, :, 1], "core", xor_perm(CORES, 1))
    blocks = jnp.stack([blocks[:, :, 0], other], axis=1).reshape(LANES, width, feats)
    return weights_out(blocks, order)[None]


def solution(mesh):
    devices = np.asarray(mesh.devices).reshape(4, 2, 2, Y, CORES)
    fine = Mesh(devices, ("z", "x_lo", "x_hi", "y", "core"))
    rep, feat = ("z", "x_lo"), ("x_hi", "y", "core")
    in_specs = (P(None, rep, feat), P(None, rep, None), P(rep, feat, None))
    return jax.shard_map(
        local, mesh=fine, in_specs=in_specs, out_specs=P(rep, feat, None), check_vma=False
    )
```

```python
import jax
import jax.numpy as jnp
import numpy as np
from jax import lax
from jax.experimental import pallas as pl
from jax.experimental.pallas import tpu as pltpu
from jax.sharding import Mesh, PartitionSpec as P

STEPS = 4
Y, CORES = 4, 2
LANES = Y * CORES
CHUNKS = 2
F32, BF16 = jnp.float32, jnp.bfloat16
VMEM_LIMIT = 48 * 2**20


def swap(x, axis, mask):
    return lax.ppermute(x, axis, [(i, i ^ mask) for i in range(lax.axis_size(axis))])


def params():
    return pltpu.CompilerParams(vmem_limit_bytes=VMEM_LIMIT)


def split(x):
    high = x.astype(BF16)
    return high, (x - high.astype(F32)).astype(BF16)


def widen(hidden):
    steps, rows, feats = hidden.shape

    def body(x_ref, o_ref):
        o_ref[...] = x_ref[...].astype(F32)

    spec = pl.BlockSpec((1, rows, feats), lambda s: (s, 0, 0))
    return pl.pallas_call(
        body,
        grid=(steps,),
        in_specs=[spec],
        out_specs=spec,
        out_shape=jax.ShapeDtypeStruct(hidden.shape, F32),
        compiler_params=params(),
    )(hidden)


def narrow(gathered, order):
    if isinstance(gathered, list):
        rows, feats = gathered[0].shape
        arrays, count = gathered, len(gathered)
    else:
        count, rows, feats = gathered.shape
        arrays = [gathered] * count
    some = rows // 4

    def body(order_ref, *refs):
        x_ref, t_ref = refs[count:]
        for k in range(count):
            block = refs[k][...].reshape(some, feats).astype(F32)
            x_ref[:, k * feats : (k + 1) * feats] = block.astype(BF16)
            t_ref[k * feats : (k + 1) * feats, :] = block.T.astype(BF16)

    if isinstance(gathered, list):
        specs = [pl.BlockSpec((some, feats), lambda i, order: (i, 0))] * count
    else:
        specs = [
            pl.BlockSpec((1, some, feats), lambda i, order, k=k: (order[k], i, 0))
            for k in range(count)
        ]
    return pl.pallas_call(
        body,
        grid_spec=pltpu.PrefetchScalarGridSpec(
            num_scalar_prefetch=1,
            grid=(rows // some,),
            in_specs=specs,
            out_specs=[
                pl.BlockSpec((some, count * feats), lambda i, order: (i, 0)),
                pl.BlockSpec((count * feats, some), lambda i, order: (0, i)),
            ],
        ),
        out_shape=[
            jax.ShapeDtypeStruct((rows, count * feats), BF16),
            jax.ShapeDtypeStruct((count * feats, rows), BF16),
        ],
        compiler_params=params(),
    )(order, *arrays)


def begin(near, far, weights):
    rows, feats = near[0].shape
    half = rows // 2
    probes = weights[0].shape[1]
    some = probes // CHUNKS
    slots = (0, 1, 2, 3, 6, 7)

    def body(*refs):
        near_refs, far_refs, w_refs = refs[:6], refs[6:10], refs[10:14]
        x_ref = refs[14]
        state_refs, margin_refs = refs[15 : 15 + CHUNKS], refs[15 + CHUNKS : 15 + 2 * CHUNKS]
        high, low = refs[-2:]

        @pl.when(pl.program_id(0) == 0)
        def _():
            for k in range(Y):
                for j in range(CORES):
                    at = slice((k * CORES + j) * feats, (k * CORES + j + 1) * feats)
                    piece = w_refs[k][j]
                    for c in range(CHUNKS):
                        state_refs[c][:, at] = piece[c * some : (c + 1) * some]
                    high[:, at], low[:, at] = split(piece)
            for j in range(CORES):
                x_ref[:, (4 + j) * feats : (5 + j) * feats] = far_refs[j][...].astype(BF16)

        @pl.when(pl.program_id(0) == 1)
        def _():
            for j in range(CORES):
                x_ref[:, (4 + j) * feats : (5 + j) * feats] = far_refs[2 + j][...].astype(BF16)

        for ref, k in zip(near_refs, slots, strict=True):
            x_ref[:, k * feats : (k + 1) * feats] = ref[...].astype(BF16)
        dims = (((1,), (1,)), ((), ()))
        x = x_ref[...]
        margin = lax.dot_general(high[...], x, dims, preferred_element_type=F32)
        margin += lax.dot_general(low[...], x, dims, preferred_element_type=F32)
        for c in range(CHUNKS):
            margin_refs[c][...] = margin[c * some : (c + 1) * some]

    wide = LANES * feats
    outs = pl.pallas_call(
        body,
        grid=(2,),
        in_specs=[pl.BlockSpec((half, feats), lambda i: (i, 0))] * 6
        + [pl.BlockSpec((half, feats), lambda i: (0, 0))] * 4
        + [pl.BlockSpec((CORES, probes, feats), lambda i: (0, 0, 0))] * 4,
        out_specs=[pl.BlockSpec((half, wide), lambda i: (i, 0))]
        + [pl.BlockSpec((some, wide), lambda i: (0, 0))] * CHUNKS
        + [pl.BlockSpec((some, half), lambda i: (0, i))] * CHUNKS,
        out_shape=[jax.ShapeDtypeStruct((rows, wide), BF16)]
        + [jax.ShapeDtypeStruct((some, wide), F32)] * CHUNKS
        + [jax.ShapeDtypeStruct((some, rows), F32)] * CHUNKS,
        scratch_shapes=[pltpu.VMEM((probes, wide), BF16)] * 2,
        compiler_params=params(),
    )(*near, *far, *weights)
    return outs[0], outs[1 : 1 + CHUNKS], outs[1 + CHUNKS :]


def weights_in(weights, order):
    feats, probes = weights.shape
    width = probes // LANES

    def body(order_ref, w_ref, own_ref, other_ref):
        for k in range(Y):
            for j, o_ref in enumerate((own_ref, other_ref)):
                start = pl.multiple_of(order_ref[k * CORES + j] * width, width)
                o_ref[k] = w_ref[:, pl.ds(start, width)].T

    shape = (Y, width, feats)
    spec = pl.BlockSpec(shape, lambda i, order: (0, 0, 0))
    return pl.pallas_call(
        body,
        grid_spec=pltpu.PrefetchScalarGridSpec(
            num_scalar_prefetch=1,
            grid=(1,),
            in_specs=[pl.BlockSpec((feats, probes), lambda i, order: (0, 0))],
            out_specs=[spec] * 2,
        ),
        out_shape=[jax.ShapeDtypeStruct(shape, F32)] * 2,
        compiler_params=params(),
    )(order, weights)


def weights_out(own, other, order):
    _, width, feats = own.shape

    def body(order_ref, own_ref, other_ref, o_ref):
        for k in range(Y):
            for j, w_ref in enumerate((own_ref, other_ref)):
                start = pl.multiple_of(order_ref[k * CORES + j] * width, width)
                o_ref[:, pl.ds(start, width)] = w_ref[k].T

    spec = pl.BlockSpec(own.shape, lambda i, order: (0, 0, 0))
    out = (feats, LANES * width)
    return pl.pallas_call(
        body,
        grid_spec=pltpu.PrefetchScalarGridSpec(
            num_scalar_prefetch=1,
            grid=(1,),
            in_specs=[spec] * 2,
            out_specs=pl.BlockSpec(out, lambda i, order: (0, 0)),
        ),
        out_shape=jax.ShapeDtypeStruct(out, F32),
        compiler_params=params(),
    )(order, own, other)


def labels_in(labels, order):
    steps, rows, probes = labels.shape
    width = probes // LANES

    def body(order_ref, l_ref, o_ref):
        o_ref[0] = l_ref[0].astype(F32).T

    return pl.pallas_call(
        body,
        grid_spec=pltpu.PrefetchScalarGridSpec(
            num_scalar_prefetch=1,
            grid=(steps,),
            in_specs=[pl.BlockSpec((1, rows, width), lambda s, order: (s, 0, order[0]))],
            out_specs=pl.BlockSpec((1, width, rows), lambda s, order: (s, 0, 0)),
        ),
        out_shape=jax.ShapeDtypeStruct((steps, width, rows), F32),
        compiler_params=params(),
    )(order, labels)


def two_pass(x, y):
    n = x.shape[0]
    high = lax.reduce_precision(x, 8, 7)
    both = jnp.concatenate([high.astype(BF16), (x - high).astype(BF16)])
    out = jnp.dot(both, y, preferred_element_type=F32)
    return out[:n] + out[n:]


def gather(x):
    half = x.shape[0] // 2
    one, three = swap(x, "y", 1), swap(x, "y", 3)
    two = [swap(one[:half], "y", 3), swap(three[half:], "y", 1)]
    return one, three, two


def after(x, *others):
    return lax.optimization_barrier((x, *others))[0]


def local(hidden, labels, weights):
    rows, feats = hidden.shape[1:]
    y, core = lax.axis_index("y"), lax.axis_index("core")
    order = jnp.arange(LANES, dtype=jnp.int32) ^ (y * CORES + core).astype(jnp.int32)

    zero = widen(hidden[:1])[0]
    one, three, two = gather(zero)
    keep, give = weights_in(weights[0], order)
    got = swap(give, "core", 1)
    pieces = jnp.stack([keep, got], axis=1)
    pieces = [pieces[0]] + [swap(pieces[k], "y", k) for k in (1, 2, 3)]

    wide = after(widen(hidden[1:]), one, three)
    later = {1: lax.all_gather(wide[0], ("y", "core"))}
    targets = labels_in(labels, order)

    near = []
    for block in (zero, one, three):
        near += [block, swap(block, "core", 1)]
    near[0] = hidden[0]
    far = []
    for block in two:
        far += [block, swap(block, "core", 1)]
    x, states, margins = begin(near, far, pieces)

    received = [swap(m, "x_hi", 1) for m in margins]
    second = after(wide[1], *received)
    one, three, two = gather(second)
    later[3] = lax.all_gather(after(wide[2], *received), ("y", "core"))

    for step in range(STEPS):
        if step in (1, 3):
            x, xt = narrow(later[step], order)
        elif step == 2:
            two = jnp.concatenate(two)
            blocks = []
            for block in (second, one, two, three):
                blocks += [block, swap(block, "core", 1)]
            blocks[0] = hidden[2]
            x, xt = narrow(blocks, order)
        if step:
            margins = [two_pass(s, xt) for s in states]
            received = [swap(m, "x_hi", 1) for m in margins]
        updates = []
        for c in range(CHUNKS):
            some = margins[c].shape[0]
            residual = jax.nn.sigmoid(margins[c] + received[c]) - targets[step, c * some : (c + 1) * some]
            updates.append(states[c] - 2.0 / rows * two_pass(residual, x))
        bit = step % 3
        partners = [swap(u, "z", bit) if bit else swap(u, "x_lo", 1) for u in updates]
        states = [0.5 * (u + p) for u, p in zip(updates, partners, strict=True)]

    deep = CORES * feats
    parts = []
    for state in states:
        parts.append(
            [state[:, :deep]] + [swap(state[:, k * deep : (k + 1) * deep], "y", k) for k in (1, 2, 3)]
        )
    blocks = jnp.stack([jnp.concatenate([part[k] for part in parts]) for k in range(Y)])
    own, give = blocks[:, :, :feats], blocks[:, :, feats:]
    return weights_out(own, swap(give, "core", 1), order)[None]


def solution(mesh):
    devices = np.asarray(mesh.devices).reshape(4, 2, 2, Y, CORES)
    fine = Mesh(devices, ("z", "x_lo", "x_hi", "y", "core"))
    rep, feat = ("z", "x_lo"), ("x_hi", "y", "core")
    in_specs = (P(None, rep, feat), P(None, rep, None), P(rep, feat, None))
    return jax.shard_map(
        local, mesh=fine, in_specs=in_specs, out_specs=P(rep, feat, None), check_vma=False
    )
```

```python
import jax
import jax.numpy as jnp
import numpy as np
from jax import lax
from jax.experimental import pallas as pl
from jax.experimental.pallas import tpu as pltpu
from jax.sharding import Mesh, PartitionSpec as P

STEPS = 4
Y, CORES = 4, 2
LANES = Y * CORES
F32, BF16 = jnp.float32, jnp.bfloat16
MIB = 2**20


def swap(x, axis, mask):
    return lax.ppermute(x, axis, [(i, i ^ mask) for i in range(lax.axis_size(axis))])


def params(mib):
    return pltpu.CompilerParams(vmem_limit_bytes=mib * MIB)


def cost(bytes_accessed, flops=0):
    return pl.CostEstimate(flops=flops, bytes_accessed=bytes_accessed, transcendentals=0)


def split(x):
    high = x.astype(BF16)
    return high, (x - high.astype(F32)).astype(BF16)


def widen(hidden, step, behind=()):
    _, rows, feats = hidden.shape

    def body(x_ref, *refs):
        refs[-1][...] = x_ref[0].astype(F32)

    return pl.pallas_call(
        body,
        grid=(2,),
        in_specs=[pl.BlockSpec((1, rows // 2, feats), lambda i: (step, i, 0))]
        + [pl.BlockSpec(memory_space=pl.ANY)] * len(behind),
        out_specs=pl.BlockSpec((rows // 2, feats), lambda i: (i, 0)),
        out_shape=jax.ShapeDtypeStruct((rows, feats), F32),
        compiler_params=params(6),
        cost_estimate=cost(6 * rows * feats),
    )(hidden, *behind)


def narrow(near, far):
    rows, feats = near[0].shape
    some, wide = rows // 4, LANES * feats
    slots = (0, 1, 2, 3, 6, 7)

    def body(*refs):
        near_refs, far_refs = refs[:6], refs[6:10]
        x_ref, t_ref = refs[10:]

        def put(k, block):
            at = slice(k * feats, (k + 1) * feats)
            x_ref[:, at] = block.astype(BF16)
            t_ref[at, :] = block.astype(F32).T.astype(BF16)

        for ref, k in zip(near_refs, slots, strict=True):
            put(k, ref[...])
        late = pl.program_id(0) >= 2
        for j in range(CORES):
            put(4 + j, jnp.where(late, far_refs[2 + j][...], far_refs[j][...]))

    return pl.pallas_call(
        body,
        grid=(rows // some,),
        in_specs=[pl.BlockSpec((some, feats), lambda i: (i, 0))] * 6
        + [pl.BlockSpec((some, feats), lambda i: (jnp.minimum(i, 1), 0))] * 2
        + [pl.BlockSpec((some, feats), lambda i: (jnp.maximum(i, 2) - 2, 0))] * 2,
        out_specs=[
            pl.BlockSpec((some, wide), lambda i: (i, 0)),
            pl.BlockSpec((wide, some), lambda i: (0, i)),
        ],
        out_shape=[
            jax.ShapeDtypeStruct((rows, wide), BF16),
            jax.ShapeDtypeStruct((wide, rows), BF16),
        ],
        compiler_params=params(14),
        cost_estimate=cost(8 * rows * wide),
    )(*near, *far)


def narrow_gathered(gathered, order):
    count, rows, feats = gathered.shape
    some = rows // 4

    def body(order_ref, *refs):
        x_ref, t_ref = refs[count:]
        for k in range(count):
            at = slice(k * feats, (k + 1) * feats)
            block = refs[k][0]
            x_ref[:, at] = block.astype(BF16)
            t_ref[at, :] = block.T.astype(BF16)

    return pl.pallas_call(
        body,
        grid_spec=pltpu.PrefetchScalarGridSpec(
            num_scalar_prefetch=1,
            grid=(rows // some,),
            in_specs=[
                pl.BlockSpec((1, some, feats), lambda i, order, k=k: (order[k], i, 0))
                for k in range(count)
            ],
            out_specs=[
                pl.BlockSpec((some, count * feats), lambda i, order: (i, 0)),
                pl.BlockSpec((count * feats, some), lambda i, order: (0, i)),
            ],
        ),
        out_shape=[
            jax.ShapeDtypeStruct((rows, count * feats), BF16),
            jax.ShapeDtypeStruct((count * feats, rows), BF16),
        ],
        compiler_params=params(14),
        cost_estimate=cost(8 * count * rows * feats),
    )(order, *[gathered] * count)


def begin(near, far, weights):
    rows, feats = near[0].shape
    half = rows // 2
    probes = weights[0].shape[1]
    wide = LANES * feats
    slots = (0, 1, 2, 3, 6, 7)

    def body(*refs):
        near_refs, far_refs, w_refs = refs[:6], refs[6:10], refs[10:14]
        x_ref, state_ref, margin_ref, high, low = refs[14:]

        @pl.when(pl.program_id(0) == 0)
        def _():
            for k in range(Y):
                for j in range(CORES):
                    at = slice((k * CORES + j) * feats, (k * CORES + j + 1) * feats)
                    piece = w_refs[k][j]
                    state_ref[:, at] = piece
                    high[:, at], low[:, at] = split(piece)
            for j in range(CORES):
                x_ref[:, (4 + j) * feats : (5 + j) * feats] = far_refs[j][...].astype(BF16)

        @pl.when(pl.program_id(0) == 1)
        def _():
            for j in range(CORES):
                x_ref[:, (4 + j) * feats : (5 + j) * feats] = far_refs[2 + j][...].astype(BF16)

        for ref, k in zip(near_refs, slots, strict=True):
            x_ref[:, k * feats : (k + 1) * feats] = ref[...].astype(BF16)
        dims = (((1,), (1,)), ((), ()))
        x = x_ref[...]
        margin = lax.dot_general(high[...], x, dims, preferred_element_type=F32)
        margin += lax.dot_general(low[...], x, dims, preferred_element_type=F32)
        margin_ref[...] = margin

    return pl.pallas_call(
        body,
        grid=(2,),
        in_specs=[pl.BlockSpec((half, feats), lambda i: (i, 0))] * 6
        + [pl.BlockSpec((half, feats), lambda i: (0, 0))] * 4
        + [pl.BlockSpec((CORES, probes, feats), lambda i: (0, 0, 0))] * 4,
        out_specs=[
            pl.BlockSpec((half, wide), lambda i: (i, 0)),
            pl.BlockSpec((probes, wide), lambda i: (0, 0)),
            pl.BlockSpec((probes, half), lambda i: (0, i)),
        ],
        out_shape=[
            jax.ShapeDtypeStruct((rows, wide), BF16),
            jax.ShapeDtypeStruct((probes, wide), F32),
            jax.ShapeDtypeStruct((probes, rows), F32),
        ],
        scratch_shapes=[pltpu.VMEM((probes, wide), BF16)] * 2,
        compiler_params=params(24),
        cost_estimate=cost(6 * rows * wide, 4 * rows * wide * probes),
    )(*near, *far, *weights)


def weights_in(weights, order):
    feats, probes = weights.shape
    width = probes // LANES

    def body(order_ref, w_ref, own_ref, other_ref):
        for k in range(Y):
            for j, o_ref in enumerate((own_ref, other_ref)):
                start = pl.multiple_of(order_ref[k * CORES + j] * width, width)
                o_ref[k] = w_ref[:, pl.ds(start, width)].T

    shape = (Y, width, feats)
    spec = pl.BlockSpec(shape, lambda i, order: (0, 0, 0))
    return pl.pallas_call(
        body,
        grid_spec=pltpu.PrefetchScalarGridSpec(
            num_scalar_prefetch=1,
            grid=(1,),
            in_specs=[pl.BlockSpec((feats, probes), lambda i, order: (0, 0))],
            out_specs=[spec] * 2,
        ),
        out_shape=[jax.ShapeDtypeStruct(shape, F32)] * 2,
        compiler_params=params(8),
    )(order, weights)


def weights_out(own, other, order):
    _, width, feats = own.shape

    def body(order_ref, own_ref, other_ref, o_ref):
        for k in range(Y):
            for j, w_ref in enumerate((own_ref, other_ref)):
                start = pl.multiple_of(order_ref[k * CORES + j] * width, width)
                o_ref[:, pl.ds(start, width)] = w_ref[k].T

    spec = pl.BlockSpec(own.shape, lambda i, order: (0, 0, 0))
    out = (feats, LANES * width)
    return pl.pallas_call(
        body,
        grid_spec=pltpu.PrefetchScalarGridSpec(
            num_scalar_prefetch=1,
            grid=(1,),
            in_specs=[spec] * 2,
            out_specs=pl.BlockSpec(out, lambda i, order: (0, 0)),
        ),
        out_shape=jax.ShapeDtypeStruct(out, F32),
        compiler_params=params(8),
    )(order, own, other)


def labels_in(labels, order):
    steps, rows, probes = labels.shape
    width = probes // LANES

    def body(order_ref, l_ref, o_ref):
        o_ref[0] = l_ref[0].astype(F32).T

    return pl.pallas_call(
        body,
        grid_spec=pltpu.PrefetchScalarGridSpec(
            num_scalar_prefetch=1,
            grid=(steps,),
            in_specs=[pl.BlockSpec((1, rows, width), lambda s, order: (s, 0, order[0]))],
            out_specs=pl.BlockSpec((1, width, rows), lambda s, order: (s, 0, 0)),
        ),
        out_shape=jax.ShapeDtypeStruct((steps, width, rows), F32),
        compiler_params=params(52),
        cost_estimate=cost(8 * steps * rows * width),
    )(order, labels)


def send_behind(x, token):
    def body(x_ref, token_ref, o_ref):
        o_ref[...] = x_ref[...]

    return pl.pallas_call(
        body,
        in_specs=[pl.BlockSpec(memory_space=pltpu.VMEM), pl.BlockSpec(memory_space=pl.ANY)],
        out_shape=jax.ShapeDtypeStruct(x.shape, x.dtype),
        compiler_params=params(4),
    )(x, token)


def two_pass(x, y):
    n = x.shape[0]
    high = lax.reduce_precision(x, 8, 7)
    both = jnp.concatenate([high.astype(BF16), (x - high).astype(BF16)])
    out = jnp.dot(both, y, preferred_element_type=F32)
    return out[:n] + out[n:]


def first_hop(x):
    return swap(x, "y", 1), swap(x, "y", 3)


def second_hop(one, three):
    half = one.shape[0] // 2
    return swap(one[:half], "y", 3), swap(three[half:], "y", 1)


def land(own, narrow_own, one, three, two):
    near = [narrow_own, swap(own, "core", 1), one, swap(one, "core", 1), three, swap(three, "core", 1)]
    far = [two[0], swap(two[0], "core", 1), two[1], swap(two[1], "core", 1)]
    return near, far


def corners(*arrays):
    return [x[:8, :128] for x in arrays]


def in_turn(x, axis):
    first, second = ([(core, 2 + core), (2 + core, core)] for core in range(CORES))
    early = lax.ppermute(x, (axis, "core"), first)
    token = lax.ppermute(early[:8, :128], "core", [(0, 1)])
    late = lax.ppermute(send_behind(x, token), (axis, "core"), second)
    return early + late


def tie(*arrays):
    return lax.optimization_barrier(arrays)


def local(hidden, labels, weights):
    rows, feats = hidden.shape[1:]
    y, core = lax.axis_index("y"), lax.axis_index("core")
    order = jnp.arange(LANES, dtype=jnp.int32) ^ (y * CORES + core).astype(jnp.int32)

    own = widen(hidden, 0)
    one, three = first_hop(own)
    keep, give = weights_in(weights[0], order)
    pieces = jnp.stack([keep, swap(give, "core", 1)], axis=1)
    pieces = [pieces[0]] + [swap(pieces[k], "y", k) for k in (1, 2, 3)]
    one, three, *pieces = tie(one, three, *pieces)
    near, far = land(own, hidden[0], one, three, second_hop(one, three))

    next_own = widen(hidden, 1)
    next_one, next_three = first_hop(next_own)
    targets = labels_in(labels, order)

    x, state, margin = begin(near, far, pieces)

    for step in range(STEPS):
        if step:
            margin = two_pass(state, xt)
        received = in_turn(margin, "x_hi") if step == 1 else swap(margin, "x_hi", 1)
        if step == 0:
            received, one, three = tie(received, next_one, next_three)
            landed = corners(received, one, three)
            later = {s: lax.all_gather(widen(hidden, s, landed), ("y", "core")) for s in (2, 3)}
        residual = jax.nn.sigmoid(margin + received) - targets[step]
        update = state - 2.0 / rows * two_pass(residual, x)
        if step + 1 == STEPS:
            break
        bit = step % 3
        partner = swap(update, "z", bit) if bit else swap(update, "x_lo", 1)
        if step == 0:
            x, xt = narrow(*land(next_own, hidden[1], one, three, second_hop(one, three)))
        else:
            x, xt = narrow_gathered(later[step + 1], order)
        state = 0.5 * (update + partner)

    deep = CORES * feats
    away, stay = update[:, deep:], update[:, :deep]
    away = 0.5 * (away + swap(away, "x_lo", 1))
    stay, away = tie(stay, away)
    blocks = [0.5 * (stay + swap(stay, "x_lo", 1))]
    blocks += [swap(away[:, (k - 1) * deep : k * deep], "y", k) for k in (1, 2, 3)]
    blocks = jnp.stack(blocks)
    own, give = blocks[:, :, :feats], blocks[:, :, feats:]
    return weights_out(own, swap(give, "core", 1), order)[None]


def solution(mesh):
    devices = np.asarray(mesh.devices).reshape(4, 2, 2, Y, CORES)
    fine = Mesh(devices, ("z", "x_lo", "x_hi", "y", "core"))
    rep, feat = ("z", "x_lo"), ("x_hi", "y", "core")
    in_specs = (P(None, rep, feat), P(None, rep, None), P(rep, feat, None))
    return jax.shard_map(
        local, mesh=fine, in_specs=in_specs, out_specs=P(rep, feat, None), check_vma=False
    )
```

```python
import jax
import jax.numpy as jnp
import numpy as np
from jax import lax
from jax.experimental import pallas as pl
from jax.experimental.pallas import tpu as pltpu
from jax.sharding import Mesh, PartitionSpec as P

STEPS = 4
Y, CORES = 4, 2
LANES = Y * CORES
F32, BF16 = jnp.float32, jnp.bfloat16
MIB = 2**20


def swap(x, axis, mask):
    return lax.ppermute(x, axis, [(i, i ^ mask) for i in range(lax.axis_size(axis))])


def swap_both(x, mask):
    return lax.ppermute(x, ("x_lo", "y"), [(i, i ^ (Y + mask)) for i in range(2 * Y)])


def params(mib):
    return pltpu.CompilerParams(vmem_limit_bytes=mib * MIB)


def cost(bytes_accessed, flops=0):
    return pl.CostEstimate(flops=flops, bytes_accessed=bytes_accessed, transcendentals=0)


def split(x):
    high = x.astype(BF16)
    return high, (x - high.astype(F32)).astype(BF16)


def widen(hidden, step):
    _, rows, feats = hidden.shape

    def body(x_ref, o_ref):
        o_ref[...] = x_ref[0].astype(F32)

    return pl.pallas_call(
        body,
        grid=(2,),
        in_specs=[pl.BlockSpec((1, rows // 2, feats), lambda i: (step, i, 0))],
        out_specs=pl.BlockSpec((rows // 2, feats), lambda i: (i, 0)),
        out_shape=jax.ShapeDtypeStruct((rows, feats), F32),
        compiler_params=params(6),
        cost_estimate=cost(6 * rows * feats),
    )(hidden)


def narrow(near, far):
    rows, feats = near[0].shape
    some, wide = rows // 4, LANES * feats
    slots = (0, 1, 2, 3, 6, 7)

    def body(*refs):
        near_refs, far_refs = refs[:6], refs[6:10]
        x_ref, t_ref = refs[10:]

        def put(k, block):
            at = slice(k * feats, (k + 1) * feats)
            x_ref[:, at] = block.astype(BF16)
            t_ref[at, :] = block.astype(F32).T.astype(BF16)

        for ref, k in zip(near_refs, slots, strict=True):
            put(k, ref[...])
        late = pl.program_id(0) >= 2
        for j in range(CORES):
            put(4 + j, jnp.where(late, far_refs[2 + j][...], far_refs[j][...]))

    return pl.pallas_call(
        body,
        grid=(rows // some,),
        in_specs=[pl.BlockSpec((some, feats), lambda i: (i, 0))] * 6
        + [pl.BlockSpec((some, feats), lambda i: (jnp.minimum(i, 1), 0))] * 2
        + [pl.BlockSpec((some, feats), lambda i: (jnp.maximum(i, 2) - 2, 0))] * 2,
        out_specs=[
            pl.BlockSpec((some, wide), lambda i: (i, 0)),
            pl.BlockSpec((wide, some), lambda i: (0, i)),
        ],
        out_shape=[
            jax.ShapeDtypeStruct((rows, wide), BF16),
            jax.ShapeDtypeStruct((wide, rows), BF16),
        ],
        compiler_params=params(14),
        cost_estimate=cost(8 * rows * wide),
    )(*near, *far)


def narrow_gathered(gathered, order):
    count, rows, feats = gathered.shape
    some = rows // 4

    def body(order_ref, *refs):
        x_ref, t_ref = refs[count:]
        for k in range(count):
            at = slice(k * feats, (k + 1) * feats)
            block = refs[k][0]
            x_ref[:, at] = block.astype(BF16)
            t_ref[at, :] = block.T.astype(BF16)

    return pl.pallas_call(
        body,
        grid_spec=pltpu.PrefetchScalarGridSpec(
            num_scalar_prefetch=1,
            grid=(rows // some,),
            in_specs=[
                pl.BlockSpec((1, some, feats), lambda i, order, k=k: (order[k], i, 0))
                for k in range(count)
            ],
            out_specs=[
                pl.BlockSpec((some, count * feats), lambda i, order: (i, 0)),
                pl.BlockSpec((count * feats, some), lambda i, order: (0, i)),
            ],
        ),
        out_shape=[
            jax.ShapeDtypeStruct((rows, count * feats), BF16),
            jax.ShapeDtypeStruct((count * feats, rows), BF16),
        ],
        compiler_params=params(14),
        cost_estimate=cost(8 * count * rows * feats),
    )(order, *[gathered] * count)


SLOTS = (0, 1, 2, 3, 6, 7)


def place(near_refs, far_refs, x_ref):
    feats = near_refs[0].shape[1]
    for ref, k in zip(near_refs, SLOTS, strict=True):
        x_ref[:, k * feats : (k + 1) * feats] = ref[...].astype(BF16)
    for half in range(2):

        @pl.when(pl.program_id(0) == half)
        def _(half=half):
            for j in range(CORES):
                at = slice((4 + j) * feats, (5 + j) * feats)
                x_ref[:, at] = far_refs[2 * half + j][...].astype(BF16)


def collect(near, far):
    rows, feats = near[0].shape
    half, wide = rows // 2, LANES * feats

    def body(*refs):
        place(refs[:6], refs[6:10], refs[10])

    return pl.pallas_call(
        body,
        grid=(2,),
        in_specs=[pl.BlockSpec((half, feats), lambda i: (i, 0))] * 6
        + [pl.BlockSpec((half, feats), lambda i: (0, 0))] * 4,
        out_specs=pl.BlockSpec((half, wide), lambda i: (i, 0)),
        out_shape=jax.ShapeDtypeStruct((rows, wide), BF16),
        compiler_params=params(16),
    )(*near, *far)


def begin(near, far, weights):
    rows, feats = near[0].shape
    half = rows // 2
    probes = weights[0].shape[1]
    wide = LANES * feats

    def body(*refs):
        near_refs, far_refs, w_refs = refs[:6], refs[6:10], refs[10:14]
        state_ref, margin_ref, x_ref, high, low = refs[14:]

        @pl.when(pl.program_id(0) == 0)
        def _():
            for k in range(Y):
                for j in range(CORES):
                    at = slice((k * CORES + j) * feats, (k * CORES + j + 1) * feats)
                    piece = w_refs[k][j]
                    state_ref[:, at] = piece
                    high[:, at], low[:, at] = split(piece)

        place(near_refs, far_refs, x_ref)
        dims = (((1,), (1,)), ((), ()))
        x = x_ref[...]
        margin = lax.dot_general(high[...], x, dims, preferred_element_type=F32)
        margin += lax.dot_general(low[...], x, dims, preferred_element_type=F32)
        margin_ref[...] = margin

    return pl.pallas_call(
        body,
        grid=(2,),
        in_specs=[pl.BlockSpec((half, feats), lambda i: (i, 0))] * 6
        + [pl.BlockSpec((half, feats), lambda i: (0, 0))] * 4
        + [pl.BlockSpec((CORES, probes, feats), lambda i: (0, 0, 0))] * 4,
        out_specs=[
            pl.BlockSpec((probes, wide), lambda i: (0, 0)),
            pl.BlockSpec((probes, half), lambda i: (0, i)),
        ],
        out_shape=[
            jax.ShapeDtypeStruct((probes, wide), F32),
            jax.ShapeDtypeStruct((probes, rows), F32),
        ],
        scratch_shapes=[pltpu.VMEM((half, wide), BF16)] + [pltpu.VMEM((probes, wide), BF16)] * 2,
        compiler_params=params(20),
    )(*near, *far, *weights)


def weights_in(weights, order):
    feats, probes = weights.shape
    width = probes // LANES

    def body(order_ref, w_ref, own_ref, other_ref):
        for k in range(Y):
            for j, o_ref in enumerate((own_ref, other_ref)):
                start = pl.multiple_of(order_ref[k * CORES + j] * width, width)
                o_ref[k] = w_ref[:, pl.ds(start, width)].T

    shape = (Y, width, feats)
    spec = pl.BlockSpec(shape, lambda i, order: (0, 0, 0))
    return pl.pallas_call(
        body,
        grid_spec=pltpu.PrefetchScalarGridSpec(
            num_scalar_prefetch=1,
            grid=(1,),
            in_specs=[pl.BlockSpec((feats, probes), lambda i, order: (0, 0))],
            out_specs=[spec] * 2,
        ),
        out_shape=[jax.ShapeDtypeStruct(shape, F32)] * 2,
        compiler_params=params(8),
    )(order, weights)


def weights_out(own, other, order):
    _, width, feats = own.shape

    def body(order_ref, own_ref, other_ref, o_ref):
        for k in range(Y):
            for j, w_ref in enumerate((own_ref, other_ref)):
                start = pl.multiple_of(order_ref[k * CORES + j] * width, width)
                o_ref[:, pl.ds(start, width)] = w_ref[k].T

    spec = pl.BlockSpec(own.shape, lambda i, order: (0, 0, 0))
    out = (feats, LANES * width)
    return pl.pallas_call(
        body,
        grid_spec=pltpu.PrefetchScalarGridSpec(
            num_scalar_prefetch=1,
            grid=(1,),
            in_specs=[spec] * 2,
            out_specs=pl.BlockSpec(out, lambda i, order: (0, 0)),
        ),
        out_shape=jax.ShapeDtypeStruct(out, F32),
        compiler_params=params(8),
    )(order, own, other)


def labels_in(labels, order):
    steps, rows, probes = labels.shape
    width = probes // LANES

    def body(order_ref, l_ref, o_ref):
        o_ref[0] = l_ref[0].astype(F32).T

    return pl.pallas_call(
        body,
        grid_spec=pltpu.PrefetchScalarGridSpec(
            num_scalar_prefetch=1,
            grid=(steps,),
            in_specs=[pl.BlockSpec((1, rows, width), lambda s, order: (s, 0, order[0]))],
            out_specs=pl.BlockSpec((1, width, rows), lambda s, order: (s, 0, 0)),
        ),
        out_shape=jax.ShapeDtypeStruct((steps, width, rows), F32),
        compiler_params=params(52),
        cost_estimate=cost(8 * steps * rows * width),
    )(order, labels)


def send_behind(x, token):
    def body(x_ref, token_ref, o_ref):
        o_ref[...] = x_ref[...]

    return pl.pallas_call(
        body,
        in_specs=[pl.BlockSpec(memory_space=pltpu.VMEM), pl.BlockSpec(memory_space=pl.ANY)],
        out_shape=jax.ShapeDtypeStruct(x.shape, x.dtype),
        compiler_params=params(4),
    )(x, token)


def two_pass(x, y):
    n = x.shape[0]
    high = lax.reduce_precision(x, 8, 7)
    both = jnp.concatenate([high.astype(BF16), (x - high).astype(BF16)])
    out = jnp.dot(both, y, preferred_element_type=F32)
    return out[:n] + out[n:]


def first_hop(x):
    return swap(x, "y", 1), swap(x, "y", 3)


def second_hop(one, three):
    half = one.shape[0] // 2
    return swap(one[:half], "y", 3), swap(three[half:], "y", 1)


def land(own, narrow_own, one, three, two):
    near = [narrow_own, swap(own, "core", 1), one, swap(one, "core", 1), three, swap(three, "core", 1)]
    far = [two[0], swap(two[0], "core", 1), two[1], swap(two[1], "core", 1)]
    return near, far


def in_turn(x, axis):
    first, second = ([(core, 2 + core), (2 + core, core)] for core in range(CORES))
    early = lax.ppermute(x, (axis, "core"), first)
    token = lax.ppermute(early[:8, :128], "core", [(0, 1)])
    late = lax.ppermute(send_behind(x, token), (axis, "core"), second)
    return early + late


def tie(*arrays):
    return lax.optimization_barrier(arrays)


def local(hidden, labels, weights):
    rows, feats = hidden.shape[1:]
    y, core = lax.axis_index("y"), lax.axis_index("core")
    order = jnp.arange(LANES, dtype=jnp.int32) ^ (y * CORES + core).astype(jnp.int32)

    own = widen(hidden, 0)
    one, three = first_hop(own)
    keep, give = weights_in(weights[0], order)
    pieces = jnp.stack([keep, swap(give, "core", 1)], axis=1)
    pieces = [pieces[0]] + [swap(pieces[k], "y", k) for k in (1, 2, 3)]
    targets = labels_in(labels, order)
    one, three, targets, *pieces = tie(one, three, targets, *pieces)
    near, far = land(own, hidden[0], one, three, second_hop(one, three))

    next_own = widen(hidden, 1)
    next_one, next_three = first_hop(next_own)
    wides = [widen(hidden, s) for s in (2, 3)]

    state, margin = begin(near, far, pieces)
    x = collect(near, far)

    for step in range(STEPS):
        if step:
            margin = two_pass(state, xt)
        received = in_turn(margin, "x_hi") if step == 1 else swap(margin, "x_hi", 1)
        if step == 0:
            received, x, one, three, *wides = tie(received, x, next_one, next_three, *wides)
            later = {s: lax.all_gather(wide, ("y", "core")) for s, wide in zip((2, 3), wides, strict=True)}
        residual = jax.nn.sigmoid(margin + received) - targets[step]
        update = state - 2.0 / rows * two_pass(residual, x)
        if step + 1 == STEPS:
            break
        bit = step % 3
        partner = swap(update, "z", bit) if bit else swap(update, "x_lo", 1)
        if step == 0:
            x, xt = narrow(*land(next_own, hidden[1], one, three, second_hop(one, three)))
        else:
            x, xt = narrow_gathered(later[step + 1], order)
            partner, x, xt = tie(partner, x, xt)
        state = 0.5 * (update + partner)

    deep = CORES * feats
    pieces = [update[:, k * deep : (k + 1) * deep] for k in range(Y)]
    landed = tie(*[swap_both(pieces[k], k) for k in (2, 1, 3, 0)], *[swap(pieces[k], "y", k) for k in (2, 1, 3)])
    mine = (*landed[4:], pieces[0])
    two, one, three, zero = (0.5 * (a + b) for a, b in zip(mine, landed[:4], strict=True))
    blocks = jnp.stack([zero, one, two, three])
    own, give = blocks[:, :, :feats], blocks[:, :, feats:]
    return weights_out(own, swap(give, "core", 1), order)[None]


def solution(mesh):
    devices = np.asarray(mesh.devices).reshape(4, 2, 2, Y, CORES)
    fine = Mesh(devices, ("z", "x_lo", "x_hi", "y", "core"))
    rep, feat = ("z", "x_lo"), ("x_hi", "y", "core")
    in_specs = (P(None, rep, feat), P(None, rep, None), P(rep, feat, None))
    return jax.shard_map(
        local, mesh=fine, in_specs=in_specs, out_specs=P(rep, feat, None), check_vma=False
    )
```

```python
import jax
import jax.numpy as jnp
import numpy as np
from jax import lax
from jax.experimental import pallas as pl
from jax.experimental.pallas import tpu as pltpu
from jax.sharding import Mesh, PartitionSpec as P

STEPS = 4
Y, CORES = 4, 2
LANES = Y * CORES
F32, BF16 = jnp.float32, jnp.bfloat16
MIB = 2**20


def swap(x, axis, mask):
    return lax.ppermute(x, axis, [(i, i ^ mask) for i in range(lax.axis_size(axis))])


def swap_both(x, mask):
    return lax.ppermute(x, ("x_lo", "y"), [(i, i ^ (Y + mask)) for i in range(2 * Y)])


def params(mib):
    return pltpu.CompilerParams(vmem_limit_bytes=mib * MIB)


def split(x):
    high = x.astype(BF16)
    return high, (x - high.astype(F32)).astype(BF16)


def widen(hidden, step):
    _, rows, feats = hidden.shape

    def body(x_ref, o_ref):
        o_ref[...] = x_ref[0].astype(F32)

    return pl.pallas_call(
        body,
        grid=(2,),
        in_specs=[pl.BlockSpec((1, rows // 2, feats), lambda i: (step, i, 0))],
        out_specs=pl.BlockSpec((rows // 2, feats), lambda i: (i, 0)),
        out_shape=jax.ShapeDtypeStruct((rows, feats), F32),
        compiler_params=params(6),
    )(hidden)


def narrow(near, far):
    rows, feats = near[0].shape
    some, wide = rows // 4, LANES * feats
    slots = (0, 1, 2, 3, 6, 7)

    def body(*refs):
        near_refs, far_refs = refs[:6], refs[6:10]
        x_ref, t_ref = refs[10:]

        def put(k, block):
            at = slice(k * feats, (k + 1) * feats)
            x_ref[:, at] = block.astype(BF16)
            t_ref[at, :] = block.astype(F32).T.astype(BF16)

        for ref, k in zip(near_refs, slots, strict=True):
            put(k, ref[...])
        late = pl.program_id(0) >= 2
        for j in range(CORES):
            put(4 + j, jnp.where(late, far_refs[2 + j][...], far_refs[j][...]))

    return pl.pallas_call(
        body,
        grid=(rows // some,),
        in_specs=[pl.BlockSpec((some, feats), lambda i: (i, 0))] * 6
        + [pl.BlockSpec((some, feats), lambda i: (jnp.minimum(i, 1), 0))] * 2
        + [pl.BlockSpec((some, feats), lambda i: (jnp.maximum(i, 2) - 2, 0))] * 2,
        out_specs=[
            pl.BlockSpec((some, wide), lambda i: (i, 0)),
            pl.BlockSpec((wide, some), lambda i: (0, i)),
        ],
        out_shape=[
            jax.ShapeDtypeStruct((rows, wide), BF16),
            jax.ShapeDtypeStruct((wide, rows), BF16),
        ],
        compiler_params=params(14),
    )(*near, *far)


def narrow_gathered(gathered, order):
    count, rows, feats = gathered.shape
    some = rows // 4

    def body(order_ref, *refs):
        x_ref, t_ref = refs[count:]
        for k in range(count):
            at = slice(k * feats, (k + 1) * feats)
            block = refs[k][0]
            x_ref[:, at] = block.astype(BF16)
            t_ref[at, :] = block.T.astype(BF16)

    return pl.pallas_call(
        body,
        grid_spec=pltpu.PrefetchScalarGridSpec(
            num_scalar_prefetch=1,
            grid=(rows // some,),
            in_specs=[
                pl.BlockSpec((1, some, feats), lambda i, order, k=k: (order[k], i, 0))
                for k in range(count)
            ],
            out_specs=[
                pl.BlockSpec((some, count * feats), lambda i, order: (i, 0)),
                pl.BlockSpec((count * feats, some), lambda i, order: (0, i)),
            ],
        ),
        out_shape=[
            jax.ShapeDtypeStruct((rows, count * feats), BF16),
            jax.ShapeDtypeStruct((count * feats, rows), BF16),
        ],
        compiler_params=params(14),
    )(order, *[gathered] * count)


def begin(near, far, weights):
    rows, feats = near[0].shape
    half = rows // 2
    probes = weights[0].shape[1]
    wide = LANES * feats
    slots = (0, 1, 2, 3, 6, 7)

    def body(*refs):
        near_refs, far_refs, w_refs = refs[:6], refs[6:10], refs[10:14]
        x_ref, state_ref, margin_ref, high, low = refs[14:]

        @pl.when(pl.program_id(0) == 0)
        def _():
            for k in range(Y):
                for j in range(CORES):
                    at = slice((k * CORES + j) * feats, (k * CORES + j + 1) * feats)
                    piece = w_refs[k][j]
                    state_ref[:, at] = piece
                    high[:, at], low[:, at] = split(piece)
            for j in range(CORES):
                x_ref[:, (4 + j) * feats : (5 + j) * feats] = far_refs[j][...].astype(BF16)

        @pl.when(pl.program_id(0) == 1)
        def _():
            for j in range(CORES):
                x_ref[:, (4 + j) * feats : (5 + j) * feats] = far_refs[2 + j][...].astype(BF16)

        for ref, k in zip(near_refs, slots, strict=True):
            x_ref[:, k * feats : (k + 1) * feats] = ref[...].astype(BF16)
        dims = (((1,), (1,)), ((), ()))
        x = x_ref[...]
        margin = lax.dot_general(high[...], x, dims, preferred_element_type=F32)
        margin += lax.dot_general(low[...], x, dims, preferred_element_type=F32)
        margin_ref[...] = margin

    return pl.pallas_call(
        body,
        grid=(2,),
        in_specs=[pl.BlockSpec((half, feats), lambda i: (i, 0))] * 6
        + [pl.BlockSpec((half, feats), lambda i: (0, 0))] * 4
        + [pl.BlockSpec((CORES, probes, feats), lambda i: (0, 0, 0))] * 4,
        out_specs=[
            pl.BlockSpec((half, wide), lambda i: (i, 0)),
            pl.BlockSpec((probes, wide), lambda i: (0, 0)),
            pl.BlockSpec((probes, half), lambda i: (0, i)),
        ],
        out_shape=[
            jax.ShapeDtypeStruct((rows, wide), BF16),
            jax.ShapeDtypeStruct((probes, wide), F32),
            jax.ShapeDtypeStruct((probes, rows), F32),
        ],
        scratch_shapes=[pltpu.VMEM((probes, wide), BF16)] * 2,
        compiler_params=params(24),
    )(*near, *far, *weights)


def weights_in(weights, order):
    feats, probes = weights.shape
    width = probes // LANES

    def body(order_ref, w_ref, own_ref, other_ref):
        for k in range(Y):
            for j, o_ref in enumerate((own_ref, other_ref)):
                start = pl.multiple_of(order_ref[k * CORES + j] * width, width)
                o_ref[k] = w_ref[:, pl.ds(start, width)].T

    shape = (Y, width, feats)
    spec = pl.BlockSpec(shape, lambda i, order: (0, 0, 0))
    return pl.pallas_call(
        body,
        grid_spec=pltpu.PrefetchScalarGridSpec(
            num_scalar_prefetch=1,
            grid=(1,),
            in_specs=[pl.BlockSpec((feats, probes), lambda i, order: (0, 0))],
            out_specs=[spec] * 2,
        ),
        out_shape=[jax.ShapeDtypeStruct(shape, F32)] * 2,
        compiler_params=params(8),
    )(order, weights)


def weights_out(own, other, order):
    _, width, feats = own.shape

    def body(order_ref, own_ref, other_ref, o_ref):
        for k in range(Y):
            for j, w_ref in enumerate((own_ref, other_ref)):
                start = pl.multiple_of(order_ref[k * CORES + j] * width, width)
                o_ref[:, pl.ds(start, width)] = w_ref[k].T

    spec = pl.BlockSpec(own.shape, lambda i, order: (0, 0, 0))
    out = (feats, LANES * width)
    return pl.pallas_call(
        body,
        grid_spec=pltpu.PrefetchScalarGridSpec(
            num_scalar_prefetch=1,
            grid=(1,),
            in_specs=[spec] * 2,
            out_specs=pl.BlockSpec(out, lambda i, order: (0, 0)),
        ),
        out_shape=jax.ShapeDtypeStruct(out, F32),
        compiler_params=params(8),
    )(order, own, other)


def labels_in(labels, order):
    steps, rows, probes = labels.shape
    width = probes // LANES

    def body(order_ref, l_ref, o_ref):
        o_ref[0] = l_ref[0].astype(F32).T

    return pl.pallas_call(
        body,
        grid_spec=pltpu.PrefetchScalarGridSpec(
            num_scalar_prefetch=1,
            grid=(steps,),
            in_specs=[pl.BlockSpec((1, rows, width), lambda s, order: (s, 0, order[0]))],
            out_specs=pl.BlockSpec((1, width, rows), lambda s, order: (s, 0, 0)),
        ),
        out_shape=jax.ShapeDtypeStruct((steps, width, rows), F32),
        compiler_params=params(52),
    )(order, labels)


def send_behind(x, token):
    def body(x_ref, token_ref, o_ref):
        o_ref[...] = x_ref[...]

    return pl.pallas_call(
        body,
        in_specs=[pl.BlockSpec(memory_space=pltpu.VMEM), pl.BlockSpec(memory_space=pl.ANY)],
        out_shape=jax.ShapeDtypeStruct(x.shape, x.dtype),
        compiler_params=params(4),
    )(x, token)


def two_pass(x, y):
    n = x.shape[0]
    high = lax.reduce_precision(x, 8, 7)
    both = jnp.concatenate([high.astype(BF16), (x - high).astype(BF16)])
    out = jnp.dot(both, y, preferred_element_type=F32)
    return out[:n] + out[n:]


def first_hop(x):
    return swap(x, "y", 1), swap(x, "y", 3)


def to_pass_on(one, three):
    half = one.shape[0] // 2
    return one[:half], three[half:]


def second_hop(upper, lower):
    return swap(upper, "y", 3), swap(lower, "y", 1)


def land(own, narrow_own, one, three, two):
    near = [narrow_own, swap(own, "core", 1), one, swap(one, "core", 1), three, swap(three, "core", 1)]
    far = [two[0], swap(two[0], "core", 1), two[1], swap(two[1], "core", 1)]
    return near, far


def in_turn(x, axis):
    first, second = ([(core, 2 + core), (2 + core, core)] for core in range(CORES))
    early = lax.ppermute(x, (axis, "core"), first)
    token = lax.ppermute(early[:8, :128], "core", [(0, 1)])
    late = lax.ppermute(send_behind(x, token), (axis, "core"), second)
    return early + late


def tie(*arrays):
    return lax.optimization_barrier(arrays)


def local(hidden, labels, weights):
    rows, feats = hidden.shape[1:]
    y, core = lax.axis_index("y"), lax.axis_index("core")
    order = jnp.arange(LANES, dtype=jnp.int32) ^ (y * CORES + core).astype(jnp.int32)

    own = widen(hidden, 0)
    one, three = first_hop(own)
    keep, give = weights_in(weights[0], order)
    pieces = jnp.stack([keep, swap(give, "core", 1)], axis=1)
    pieces = [pieces[0]] + [swap(pieces[k], "y", k) for k in (1, 2, 3)]
    targets = labels_in(labels, order)
    next_own, upper, lower, targets, *pieces = tie(widen(hidden, 1), *to_pass_on(one, three), targets, *pieces)
    near, far = land(own, hidden[0], one, three, second_hop(upper, lower))

    next_one, next_three = first_hop(next_own)
    wides = [widen(hidden, s) for s in (2, 3)]

    x, state, margin = begin(near, far, pieces)

    for step in range(STEPS):
        if step:
            margin = two_pass(state, xt)
        received = in_turn(margin, "x_hi") if step == 1 else swap(margin, "x_hi", 1)
        if step == 0:
            received, one, three, *wides = tie(received, next_one, next_three, *wides)
            later = {s: lax.all_gather(wide, ("y", "core")) for s, wide in zip((2, 3), wides, strict=True)}
        residual = jax.nn.sigmoid(margin + received) - targets[step]
        update = state - 2.0 / rows * two_pass(residual, x)
        if step + 1 == STEPS:
            break
        bit = step % 3
        partner = swap(update, "z", bit) if bit else swap(update, "x_lo", 1)
        if step == 0:
            x, xt = narrow(*land(next_own, hidden[1], one, three, second_hop(*to_pass_on(one, three))))
        else:
            x, xt = narrow_gathered(later[step + 1], order)
            partner, x, xt = tie(partner, x, xt)
        state = 0.5 * (update + partner)

    deep = CORES * feats
    pieces = [update[:, k * deep : (k + 1) * deep] for k in range(Y)]
    landed = tie(*[swap_both(pieces[k], k) for k in (2, 1, 3, 0)], *[swap(pieces[k], "y", k) for k in (2, 1, 3)])
    mine = (*landed[4:], pieces[0])
    two, one, three, zero = (0.5 * (a + b) for a, b in zip(mine, landed[:4], strict=True))
    blocks = jnp.stack([zero, one, two, three])
    own, give = blocks[:, :, :feats], blocks[:, :, feats:]
    return weights_out(own, swap(give, "core", 1), order)[None]


def solution(mesh):
    devices = np.asarray(mesh.devices).reshape(4, 2, 2, Y, CORES)
    fine = Mesh(devices, ("z", "x_lo", "x_hi", "y", "core"))
    rep, feat = ("z", "x_lo"), ("x_hi", "y", "core")
    in_specs = (P(None, rep, feat), P(None, rep, None), P(rep, feat, None))
    return jax.shard_map(
        local, mesh=fine, in_specs=in_specs, out_specs=P(rep, feat, None), check_vma=False
    )
```

```python
import jax
import jax.numpy as jnp
import numpy as np
from jax import lax
from jax.experimental import pallas as pl
from jax.experimental.pallas import tpu as pltpu
from jax.sharding import Mesh, PartitionSpec as P

STEPS = 4
Y, CORES = 4, 2
LANES = Y * CORES
F32, BF16 = jnp.float32, jnp.bfloat16
MIB = 2**20


def swap(x, axis, mask):
    return lax.ppermute(x, axis, [(i, i ^ mask) for i in range(lax.axis_size(axis))])


def swap_both(x, mask):
    return lax.ppermute(x, ("x_lo", "y"), [(i, i ^ (Y + mask)) for i in range(2 * Y)])


def params(mib):
    return pltpu.CompilerParams(vmem_limit_bytes=mib * MIB)


def split(x):
    high = x.astype(BF16)
    return high, (x - high.astype(F32)).astype(BF16)


def widen(hidden, step):
    _, rows, feats = hidden.shape

    def body(x_ref, o_ref):
        o_ref[...] = x_ref[0].astype(F32)

    return pl.pallas_call(
        body,
        grid=(2,),
        in_specs=[pl.BlockSpec((1, rows // 2, feats), lambda i: (step, i, 0))],
        out_specs=pl.BlockSpec((rows // 2, feats), lambda i: (i, 0)),
        out_shape=jax.ShapeDtypeStruct((rows, feats), F32),
        compiler_params=params(6),
    )(hidden)


def narrow(near, far):
    rows, feats = near[0].shape
    some, wide = rows // 4, LANES * feats
    slots = (0, 1, 2, 3, 6, 7)

    def body(*refs):
        near_refs, far_refs = refs[:6], refs[6:10]
        x_ref, t_ref = refs[10:]

        def put(k, block):
            at = slice(k * feats, (k + 1) * feats)
            x_ref[:, at] = block.astype(BF16)
            t_ref[at, :] = block.astype(F32).T.astype(BF16)

        for ref, k in zip(near_refs, slots, strict=True):
            put(k, ref[...])
        late = pl.program_id(0) >= 2
        for j in range(CORES):
            put(4 + j, jnp.where(late, far_refs[2 + j][...], far_refs[j][...]))

    return pl.pallas_call(
        body,
        grid=(rows // some,),
        in_specs=[pl.BlockSpec((some, feats), lambda i: (i, 0))] * 6
        + [pl.BlockSpec((some, feats), lambda i: (jnp.minimum(i, 1), 0))] * 2
        + [pl.BlockSpec((some, feats), lambda i: (jnp.maximum(i, 2) - 2, 0))] * 2,
        out_specs=[
            pl.BlockSpec((some, wide), lambda i: (i, 0)),
            pl.BlockSpec((wide, some), lambda i: (0, i)),
        ],
        out_shape=[
            jax.ShapeDtypeStruct((rows, wide), BF16),
            jax.ShapeDtypeStruct((wide, rows), BF16),
        ],
        compiler_params=params(14),
    )(*near, *far)


def narrow_gathered(gathered, order, blocks, mib):
    count, rows, feats = gathered.shape
    some = rows // blocks

    def body(order_ref, *refs):
        x_ref, t_ref = refs[count:]
        for k in range(count):
            at = slice(k * feats, (k + 1) * feats)
            block = refs[k][0]
            x_ref[:, at] = block.astype(BF16)
            t_ref[at, :] = block.T.astype(BF16)

    return pl.pallas_call(
        body,
        grid_spec=pltpu.PrefetchScalarGridSpec(
            num_scalar_prefetch=1,
            grid=(rows // some,),
            in_specs=[
                pl.BlockSpec((1, some, feats), lambda i, order, k=k: (order[k], i, 0))
                for k in range(count)
            ],
            out_specs=[
                pl.BlockSpec((some, count * feats), lambda i, order: (i, 0)),
                pl.BlockSpec((count * feats, some), lambda i, order: (0, i)),
            ],
        ),
        out_shape=[
            jax.ShapeDtypeStruct((rows, count * feats), BF16),
            jax.ShapeDtypeStruct((count * feats, rows), BF16),
        ],
        compiler_params=params(mib),
    )(order, *[gathered] * count)


def begin(near, far, weights):
    rows, feats = near[0].shape
    half = rows // 2
    probes = weights[0].shape[1]
    wide = LANES * feats
    slots = (0, 1, 2, 3, 6, 7)

    def body(*refs):
        near_refs, far_refs, w_refs = refs[:6], refs[6:10], refs[10:14]
        x_ref, state_ref, margin_ref, high, low = refs[14:]

        @pl.when(pl.program_id(0) == 0)
        def _():
            for k in range(Y):
                for j in range(CORES):
                    at = slice((k * CORES + j) * feats, (k * CORES + j + 1) * feats)
                    piece = w_refs[k][j]
                    state_ref[:, at] = piece
                    high[:, at], low[:, at] = split(piece)
            for j in range(CORES):
                x_ref[:, (4 + j) * feats : (5 + j) * feats] = far_refs[j][...].astype(BF16)

        @pl.when(pl.program_id(0) == 1)
        def _():
            for j in range(CORES):
                x_ref[:, (4 + j) * feats : (5 + j) * feats] = far_refs[2 + j][...].astype(BF16)

        for ref, k in zip(near_refs, slots, strict=True):
            x_ref[:, k * feats : (k + 1) * feats] = ref[...].astype(BF16)
        dims = (((1,), (1,)), ((), ()))
        x = x_ref[...]
        margin = lax.dot_general(high[...], x, dims, preferred_element_type=F32)
        margin += lax.dot_general(low[...], x, dims, preferred_element_type=F32)
        margin_ref[...] = margin

    return pl.pallas_call(
        body,
        grid=(2,),
        in_specs=[pl.BlockSpec((half, feats), lambda i: (i, 0))] * 6
        + [pl.BlockSpec((half, feats), lambda i: (0, 0))] * 4
        + [pl.BlockSpec((CORES, probes, feats), lambda i: (0, 0, 0))] * 4,
        out_specs=[
            pl.BlockSpec((half, wide), lambda i: (i, 0)),
            pl.BlockSpec((probes, wide), lambda i: (0, 0)),
            pl.BlockSpec((probes, half), lambda i: (0, i)),
        ],
        out_shape=[
            jax.ShapeDtypeStruct((rows, wide), BF16),
            jax.ShapeDtypeStruct((probes, wide), F32),
            jax.ShapeDtypeStruct((probes, rows), F32),
        ],
        scratch_shapes=[pltpu.VMEM((probes, wide), BF16)] * 2,
        compiler_params=params(24),
    )(*near, *far, *weights)


def weights_in(weights, order):
    feats, probes = weights.shape
    width = probes // LANES

    def body(order_ref, w_ref, own_ref, other_ref):
        for k in range(Y):
            for j, o_ref in enumerate((own_ref, other_ref)):
                start = pl.multiple_of(order_ref[k * CORES + j] * width, width)
                o_ref[k] = w_ref[:, pl.ds(start, width)].T

    shape = (Y, width, feats)
    spec = pl.BlockSpec(shape, lambda i, order: (0, 0, 0))
    return pl.pallas_call(
        body,
        grid_spec=pltpu.PrefetchScalarGridSpec(
            num_scalar_prefetch=1,
            grid=(1,),
            in_specs=[pl.BlockSpec((feats, probes), lambda i, order: (0, 0))],
            out_specs=[spec] * 2,
        ),
        out_shape=[jax.ShapeDtypeStruct(shape, F32)] * 2,
        compiler_params=params(8),
    )(order, weights)


def weights_out(own, other, order):
    _, width, feats = own.shape

    def body(order_ref, own_ref, other_ref, o_ref):
        for k in range(Y):
            for j, w_ref in enumerate((own_ref, other_ref)):
                start = pl.multiple_of(order_ref[k * CORES + j] * width, width)
                o_ref[:, pl.ds(start, width)] = w_ref[k].T

    spec = pl.BlockSpec(own.shape, lambda i, order: (0, 0, 0))
    out = (feats, LANES * width)
    return pl.pallas_call(
        body,
        grid_spec=pltpu.PrefetchScalarGridSpec(
            num_scalar_prefetch=1,
            grid=(1,),
            in_specs=[spec] * 2,
            out_specs=pl.BlockSpec(out, lambda i, order: (0, 0)),
        ),
        out_shape=jax.ShapeDtypeStruct(out, F32),
        compiler_params=params(8),
    )(order, own, other)


def labels_in(labels, order):
    steps, rows, probes = labels.shape
    width = probes // LANES

    def body(order_ref, l_ref, o_ref):
        o_ref[0] = l_ref[0].astype(F32).T

    return pl.pallas_call(
        body,
        grid_spec=pltpu.PrefetchScalarGridSpec(
            num_scalar_prefetch=1,
            grid=(steps,),
            in_specs=[pl.BlockSpec((1, rows, width), lambda s, order: (s, 0, order[0]))],
            out_specs=pl.BlockSpec((1, width, rows), lambda s, order: (s, 0, 0)),
        ),
        out_shape=jax.ShapeDtypeStruct((steps, width, rows), F32),
        compiler_params=params(52),
    )(order, labels)


def send_behind(x, token):
    def body(x_ref, token_ref, o_ref):
        o_ref[...] = x_ref[...]

    return pl.pallas_call(
        body,
        in_specs=[pl.BlockSpec(memory_space=pltpu.VMEM), pl.BlockSpec(memory_space=pl.ANY)],
        out_shape=jax.ShapeDtypeStruct(x.shape, x.dtype),
        compiler_params=params(4),
    )(x, token)


def two_pass(x, y):
    n = x.shape[0]
    high = lax.reduce_precision(x, 8, 7)
    both = jnp.concatenate([high.astype(BF16), (x - high).astype(BF16)])
    out = jnp.dot(both, y, preferred_element_type=F32)
    return out[:n] + out[n:]


def first_hop(x):
    return swap(x, "y", 1), swap(x, "y", 3)


def to_pass_on(one, three):
    half = one.shape[0] // 2
    return one[:half], three[half:]


def second_hop(upper, lower):
    return swap(upper, "y", 3), swap(lower, "y", 1)


def land(own, narrow_own, one, three, two):
    near = [narrow_own, swap(own, "core", 1), one, swap(one, "core", 1), three, swap(three, "core", 1)]
    far = [two[0], swap(two[0], "core", 1), two[1], swap(two[1], "core", 1)]
    return near, far


def in_turn(x, axis):
    first, second = ([(core, 2 + core), (2 + core, core)] for core in range(CORES))
    early = lax.ppermute(x, (axis, "core"), first)
    token = lax.ppermute(early[:8, :128], "core", [(0, 1)])
    late = lax.ppermute(send_behind(x, token), (axis, "core"), second)
    return early + late


def tie(*arrays):
    return lax.optimization_barrier(arrays)


def local(hidden, labels, weights):
    rows, feats = hidden.shape[1:]
    y, core = lax.axis_index("y"), lax.axis_index("core")
    order = jnp.arange(LANES, dtype=jnp.int32) ^ (y * CORES + core).astype(jnp.int32)

    own = widen(hidden, 0)
    one, three = first_hop(own)
    keep, give = weights_in(weights[0], order)
    pieces = jnp.stack([keep, swap(give, "core", 1)], axis=1)
    pieces = [pieces[0]] + [swap(pieces[k], "y", k) for k in (1, 2, 3)]
    targets = labels_in(labels, order)
    next_own, upper, lower, targets, *pieces = tie(widen(hidden, 1), *to_pass_on(one, three), targets, *pieces)
    near, far = land(own, hidden[0], one, three, second_hop(upper, lower))

    next_one, next_three = first_hop(next_own)
    wides = [widen(hidden, s) for s in (2, 3)]

    x, state, margin = begin(near, far, pieces)

    for step in range(STEPS):
        if step:
            margin = two_pass(state, xt)
        received = in_turn(margin, "x_hi") if step == 1 else swap(margin, "x_hi", 1)
        if step == 0:
            received, one, three, *wides = tie(received, next_one, next_three, *wides)
            later = {s: lax.all_gather(wide, ("y", "core")) for s, wide in zip((2, 3), wides, strict=True)}
        residual = jax.nn.sigmoid(margin + received) - targets[step]
        update = state - 2.0 / rows * two_pass(residual, x)
        if step + 1 == STEPS:
            break
        bit = step % 3
        partner = swap(update, "z", bit) if bit else swap(update, "x_lo", 1)
        if step == 0:
            x, xt = narrow(*land(next_own, hidden[1], one, three, second_hop(*to_pass_on(one, three))))
        else:
            x, xt = narrow_gathered(later[step + 1], order, 4 if step == 1 else 2, 14 if step == 1 else 44)
            partner, x, xt = tie(partner, x, xt)
        state = 0.5 * (update + partner)

    deep = CORES * feats
    pieces = [update[:, k * deep : (k + 1) * deep] for k in range(Y)]
    far = swap(pieces[2], "y", 2)
    landed = tie(
        *[swap_both(pieces[k], k) for k in (1, 3, 0)],
        *[swap(pieces[k], "y", k) for k in (1, 3)],
        swap(far, "x_lo", 1),
    )
    one, three, zero, two = (
        0.5 * (a + b) for a, b in zip((*landed[3:5], pieces[0], far), (*landed[:3], landed[5]), strict=True)
    )
    blocks = jnp.stack([zero, one, two, three])
    own, give = blocks[:, :, :feats], blocks[:, :, feats:]
    return weights_out(own, swap(give, "core", 1), order)[None]


def solution(mesh):
    devices = np.asarray(mesh.devices).reshape(4, 2, 2, Y, CORES)
    fine = Mesh(devices, ("z", "x_lo", "x_hi", "y", "core"))
    rep, feat = ("z", "x_lo"), ("x_hi", "y", "core")
    in_specs = (P(None, rep, feat), P(None, rep, None), P(rep, feat, None))
    return jax.shard_map(
        local, mesh=fine, in_specs=in_specs, out_specs=P(rep, feat, None), check_vma=False
    )
```

```python
import jax
import jax.numpy as jnp
import numpy as np
from jax import lax
from jax.experimental import pallas as pl
from jax.experimental.pallas import tpu as pltpu
from jax.sharding import Mesh, PartitionSpec as P

STEPS = 4
Y, CORES = 4, 2
LANES = Y * CORES
F32, BF16 = jnp.float32, jnp.bfloat16
MIB = 2**20


def swap(x, axis, mask):
    return lax.ppermute(x, axis, [(i, i ^ mask) for i in range(lax.axis_size(axis))])


def swap_both(x, mask):
    return lax.ppermute(x, ("x_lo", "y"), [(i, i ^ (Y + mask)) for i in range(2 * Y)])


def params(mib):
    return pltpu.CompilerParams(vmem_limit_bytes=mib * MIB)


def split(x):
    high = x.astype(BF16)
    return high, (x - high.astype(F32)).astype(BF16)


def widen(hidden, step):
    _, rows, feats = hidden.shape

    def body(x_ref, o_ref):
        o_ref[...] = x_ref[0].astype(F32)

    return pl.pallas_call(
        body,
        grid=(2,),
        in_specs=[pl.BlockSpec((1, rows // 2, feats), lambda i: (step, i, 0))],
        out_specs=pl.BlockSpec((rows // 2, feats), lambda i: (i, 0)),
        out_shape=jax.ShapeDtypeStruct((rows, feats), F32),
        compiler_params=params(6),
    )(hidden)


def narrow(near, far):
    rows, feats = near[0].shape
    some, wide = rows // 4, LANES * feats
    slots = (0, 1, 2, 3, 6, 7)

    def body(*refs):
        near_refs, far_refs = refs[:6], refs[6:10]
        x_ref, t_ref = refs[10:]

        def put(k, block):
            at = slice(k * feats, (k + 1) * feats)
            x_ref[:, at] = block.astype(BF16)
            t_ref[at, :] = block.astype(F32).T.astype(BF16)

        for ref, k in zip(near_refs, slots, strict=True):
            put(k, ref[...])
        late = pl.program_id(0) >= 2
        for j in range(CORES):
            put(4 + j, jnp.where(late, far_refs[2 + j][...], far_refs[j][...]))

    return pl.pallas_call(
        body,
        grid=(rows // some,),
        in_specs=[pl.BlockSpec((some, feats), lambda i: (i, 0))] * 6
        + [pl.BlockSpec((some, feats), lambda i: (jnp.minimum(i, 1), 0))] * 2
        + [pl.BlockSpec((some, feats), lambda i: (jnp.maximum(i, 2) - 2, 0))] * 2,
        out_specs=[
            pl.BlockSpec((some, wide), lambda i: (i, 0)),
            pl.BlockSpec((wide, some), lambda i: (0, i)),
        ],
        out_shape=[
            jax.ShapeDtypeStruct((rows, wide), BF16),
            jax.ShapeDtypeStruct((wide, rows), BF16),
        ],
        compiler_params=params(14),
    )(*near, *far)


def narrow_gathered(gathered, order, blocks, mib):
    count, rows, feats = gathered.shape
    some = rows // blocks

    def body(order_ref, *refs):
        x_ref, t_ref = refs[count:]
        for k in range(count):
            at = slice(k * feats, (k + 1) * feats)
            block = refs[k][0]
            x_ref[:, at] = block.astype(BF16)
            t_ref[at, :] = block.T.astype(BF16)

    return pl.pallas_call(
        body,
        grid_spec=pltpu.PrefetchScalarGridSpec(
            num_scalar_prefetch=1,
            grid=(rows // some,),
            in_specs=[
                pl.BlockSpec((1, some, feats), lambda i, order, k=k: (order[k], i, 0))
                for k in range(count)
            ],
            out_specs=[
                pl.BlockSpec((some, count * feats), lambda i, order: (i, 0)),
                pl.BlockSpec((count * feats, some), lambda i, order: (0, i)),
            ],
        ),
        out_shape=[
            jax.ShapeDtypeStruct((rows, count * feats), BF16),
            jax.ShapeDtypeStruct((count * feats, rows), BF16),
        ],
        compiler_params=params(mib),
    )(order, *[gathered] * count)


def begin(near, far, weights):
    rows, feats = near[0].shape
    half = rows // 2
    probes = weights[0].shape[1]
    wide = LANES * feats
    slots = (0, 1, 2, 3, 6, 7)

    def body(*refs):
        near_refs, far_refs, w_refs = refs[:6], refs[6:10], refs[10:14]
        x_ref, state_ref, margin_ref, high, low = refs[14:]

        @pl.when(pl.program_id(0) == 0)
        def _():
            for k in range(Y):
                for j in range(CORES):
                    at = slice((k * CORES + j) * feats, (k * CORES + j + 1) * feats)
                    piece = w_refs[k][j]
                    state_ref[:, at] = piece
                    high[:, at], low[:, at] = split(piece)
            for j in range(CORES):
                x_ref[:, (4 + j) * feats : (5 + j) * feats] = far_refs[j][...].astype(BF16)

        @pl.when(pl.program_id(0) == 1)
        def _():
            for j in range(CORES):
                x_ref[:, (4 + j) * feats : (5 + j) * feats] = far_refs[2 + j][...].astype(BF16)

        for ref, k in zip(near_refs, slots, strict=True):
            x_ref[:, k * feats : (k + 1) * feats] = ref[...].astype(BF16)
        dims = (((1,), (1,)), ((), ()))
        x = x_ref[...]
        margin = lax.dot_general(high[...], x, dims, preferred_element_type=F32)
        margin += lax.dot_general(low[...], x, dims, preferred_element_type=F32)
        margin_ref[...] = margin

    return pl.pallas_call(
        body,
        grid=(2,),
        in_specs=[pl.BlockSpec((half, feats), lambda i: (i, 0))] * 6
        + [pl.BlockSpec((half, feats), lambda i: (0, 0))] * 4
        + [pl.BlockSpec((CORES, probes, feats), lambda i: (0, 0, 0))] * 4,
        out_specs=[
            pl.BlockSpec((half, wide), lambda i: (i, 0)),
            pl.BlockSpec((probes, wide), lambda i: (0, 0)),
            pl.BlockSpec((probes, half), lambda i: (0, i)),
        ],
        out_shape=[
            jax.ShapeDtypeStruct((rows, wide), BF16),
            jax.ShapeDtypeStruct((probes, wide), F32),
            jax.ShapeDtypeStruct((probes, rows), F32),
        ],
        scratch_shapes=[pltpu.VMEM((probes, wide), BF16)] * 2,
        compiler_params=params(24),
    )(*near, *far, *weights)


def weights_in(weights, order):
    feats, probes = weights.shape
    width = probes // LANES

    def body(order_ref, w_ref, own_ref, other_ref):
        for k in range(Y):
            for j, o_ref in enumerate((own_ref, other_ref)):
                start = pl.multiple_of(order_ref[k * CORES + j] * width, width)
                o_ref[k] = w_ref[:, pl.ds(start, width)].T

    shape = (Y, width, feats)
    spec = pl.BlockSpec(shape, lambda i, order: (0, 0, 0))
    return pl.pallas_call(
        body,
        grid_spec=pltpu.PrefetchScalarGridSpec(
            num_scalar_prefetch=1,
            grid=(1,),
            in_specs=[pl.BlockSpec((feats, probes), lambda i, order: (0, 0))],
            out_specs=[spec] * 2,
        ),
        out_shape=[jax.ShapeDtypeStruct(shape, F32)] * 2,
        compiler_params=params(8),
    )(order, weights)


def weights_out(own, other, order):
    _, width, feats = own.shape

    def body(order_ref, own_ref, other_ref, o_ref):
        for k in range(Y):
            for j, w_ref in enumerate((own_ref, other_ref)):
                start = pl.multiple_of(order_ref[k * CORES + j] * width, width)
                o_ref[:, pl.ds(start, width)] = w_ref[k].T

    spec = pl.BlockSpec((Y, width, feats // 2), lambda i, order: (0, 0, i))
    out = (feats, LANES * width)
    return pl.pallas_call(
        body,
        grid_spec=pltpu.PrefetchScalarGridSpec(
            num_scalar_prefetch=1,
            grid=(2,),
            in_specs=[spec] * 2,
            out_specs=pl.BlockSpec((feats // 2, LANES * width), lambda i, order: (i, 0)),
        ),
        out_shape=jax.ShapeDtypeStruct(out, F32),
        compiler_params=params(8),
    )(order, own, other)


def labels_in(labels, order):
    steps, rows, probes = labels.shape
    width = probes // LANES

    def body(order_ref, l_ref, o_ref):
        o_ref[0] = l_ref[0].astype(F32).T

    return pl.pallas_call(
        body,
        grid_spec=pltpu.PrefetchScalarGridSpec(
            num_scalar_prefetch=1,
            grid=(steps,),
            in_specs=[pl.BlockSpec((1, rows, width), lambda s, order: (s, 0, order[0]))],
            out_specs=pl.BlockSpec((1, width, rows), lambda s, order: (s, 0, 0)),
        ),
        out_shape=jax.ShapeDtypeStruct((steps, width, rows), F32),
        compiler_params=params(52),
    )(order, labels)


def send_behind(x, token):
    def body(x_ref, token_ref, o_ref):
        o_ref[...] = x_ref[...]

    return pl.pallas_call(
        body,
        in_specs=[pl.BlockSpec(memory_space=pltpu.VMEM), pl.BlockSpec(memory_space=pl.ANY)],
        out_shape=jax.ShapeDtypeStruct(x.shape, x.dtype),
        compiler_params=params(4),
    )(x, token)


def two_pass(x, y):
    n = x.shape[0]
    high = lax.reduce_precision(x, 8, 7)
    both = jnp.concatenate([high.astype(BF16), (x - high).astype(BF16)])
    out = jnp.dot(both, y, preferred_element_type=F32)
    return out[:n] + out[n:]


def first_hop(x):
    return swap(x, "y", 1), swap(x, "y", 3)


def to_pass_on(one, three):
    half = one.shape[0] // 2
    return one[:half], three[half:]


def second_hop(upper, lower):
    return swap(upper, "y", 3), swap(lower, "y", 1)


def land(own, narrow_own, one, three, two):
    near = [narrow_own, swap(own, "core", 1), one, swap(one, "core", 1), three, swap(three, "core", 1)]
    far = [two[0], swap(two[0], "core", 1), two[1], swap(two[1], "core", 1)]
    return near, far


def in_turn(x, axis):
    first, second = ([(core, 2 + core), (2 + core, core)] for core in range(CORES))
    early = lax.ppermute(x, (axis, "core"), first)
    token = lax.ppermute(early[:8, :128], "core", [(0, 1)])
    late = lax.ppermute(send_behind(x, token), (axis, "core"), second)
    return early + late


def tie(*arrays):
    return lax.optimization_barrier(arrays)


def local(hidden, labels, weights):
    rows, feats = hidden.shape[1:]
    y, core = lax.axis_index("y"), lax.axis_index("core")
    order = jnp.arange(LANES, dtype=jnp.int32) ^ (y * CORES + core).astype(jnp.int32)

    own = widen(hidden, 0)
    one, three = first_hop(own)
    keep, give = weights_in(weights[0], order)
    pieces = jnp.stack([keep, swap(give, "core", 1)], axis=1)
    pieces = [pieces[0]] + [swap(pieces[k], "y", k) for k in (1, 2, 3)]
    targets = labels_in(labels, order)
    next_own, upper, lower, targets, *pieces = tie(widen(hidden, 1), *to_pass_on(one, three), targets, *pieces)
    near, far = land(own, hidden[0], one, three, second_hop(upper, lower))

    next_one, next_three = first_hop(next_own)
    wides = [widen(hidden, s) for s in (2, 3)]

    x, state, margin = begin(near, far, pieces)

    for step in range(STEPS):
        if step:
            margin = two_pass(state, xt)
        received = in_turn(margin, "x_hi") if step == 1 else swap(margin, "x_hi", 1)
        if step == 0:
            received, one, three, *wides = tie(received, next_one, next_three, *wides)
            later = {s: lax.all_gather(wide, ("y", "core")) for s, wide in zip((2, 3), wides, strict=True)}
        residual = jax.nn.sigmoid(margin + received) - targets[step]
        update = state - 2.0 / rows * two_pass(residual, x)
        if step + 1 == STEPS:
            break
        bit = step % 3
        partner = swap(update, "z", bit) if bit else swap(update, "x_lo", 1)
        if step == 0:
            x, xt = narrow(*land(next_own, hidden[1], one, three, second_hop(*to_pass_on(one, three))))
        else:
            x, xt = narrow_gathered(later[step + 1], order, 4 if step == 1 else 2, 14 if step == 1 else 44)
            partner, x, xt = tie(partner, x, xt)
        state = 0.5 * (update + partner)

    deep = CORES * feats
    pieces = [update[:, k * deep : (k + 1) * deep] for k in range(Y)]
    far = swap(pieces[2], "y", 2)
    landed = tie(
        *[swap_both(pieces[k], k) for k in (1, 3, 0)],
        *[swap(pieces[k], "y", k) for k in (1, 3)],
        swap(far, "x_lo", 1),
    )
    one, three, zero, two = (
        0.5 * (a + b) for a, b in zip((*landed[3:5], pieces[0], far), (*landed[:3], landed[5]), strict=True)
    )
    blocks = jnp.stack([zero, one, two, three])
    own, give = blocks[:, :, :feats], blocks[:, :, feats:]
    return weights_out(own, swap(give, "core", 1), order)[None]


def solution(mesh):
    devices = np.asarray(mesh.devices).reshape(4, 2, 2, Y, CORES)
    fine = Mesh(devices, ("z", "x_lo", "x_hi", "y", "core"))
    rep, feat = ("z", "x_lo"), ("x_hi", "y", "core")
    in_specs = (P(None, rep, feat), P(None, rep, None), P(rep, feat, None))
    return jax.shard_map(
        local, mesh=fine, in_specs=in_specs, out_specs=P(rep, feat, None), check_vma=False
    )
```
